512 devices in a mesh: dp: 64 (over y, z), mp: 8 (over x, core).
Axes of the slice: x: 4, y: 4, z: 16, core: 2. Of those that a mesh axis runs over, the one named last changes fastest.
Arguments:
- gradient: bfloat16 [8, 64, 512, 512], P('mp', None, 'dp'), may hold values from -80 to 80
- left_root: bfloat16 [8, 64, 512, 512], P('mp', 'dp'), may hold values from -1 to 4
- right_root: bfloat16 [8, 64, 512, 512], P('mp', 'dp'), may hold values from -1 to 4
- slot_table: int32 [8, 64], P('mp'), may hold values from 0 to 63, each once within a row
- overflow: int32 [8, 64, 64], P('mp', None, 'dp'), may hold values 0 or 1
Outputs:
- update: bfloat16 [8, 64, 512, 512], P('mp', None, 'dp')
The draws below stay inside these ranges and needn't reach their ends.
Inputs may be any that keep to these rules, and one draw needn't show every extreme that they name: `slot_table`: each row names every slot 0 to 63 once; slot s of group g is held by the device of index s along dp.
All inputs are finite; a program needn't handle non-finite values. No bound on the sum of `overflow` on one device may be relied on, other than what follows from the above.
Results may differ from the reference program's by a relative error of at most 0.0049.
Values may be sent and summed in bfloat16 or wider, within the bound.
No kernel may reach another device: no remote copies, remote signals or barrier semaphores. Data moves between devices by JAX's collectives and lax.ppermute only.
A program may use at most 64 MiB of HBM per device.

```python
import math
import jax
import jax.numpy as jnp
from jax import lax

BS = 512
GROUPS = 8
SLOTS = 64
BLOCKS = 512
N_DP = 64


def make_root(key):
    key_off, key_diag = jax.random.split(key)
    shape = (GROUPS, SLOTS, BS, BS)
    raw = jax.random.uniform(key_off, shape, jnp.float32, -1.0, 1.0) * (1.7320508 / BS ** 0.5)
    symmetric = 0.5 * (raw + jnp.swapaxes(raw, 2, 3))
    diag_vals = jax.random.uniform(key_diag, (GROUPS, SLOTS, BS, 1), jnp.float32, 1.5, 3.0)
    return symmetric + jnp.eye(BS, dtype=jnp.float32) * diag_vals


def draw_gradient(key, part):
    key = jax.random.fold_in(key, 1)
    key_base, key_rows, key_cols = jax.random.split(key, 3)
    shape = (GROUPS, SLOTS, BS, BS)
    base = jnp.clip(jax.random.normal(key_base, shape, jnp.float32), -4.0, 4.0)
    rising = 3.0 ** (0.5 * jnp.arange(BS, dtype=jnp.float32) / (BS - 1))
    row_scale = 10.0 ** (0.5 * jax.random.uniform(key_rows, (GROUPS, SLOTS, BS, 1), jnp.float32)) * rising[:, None]
    col_scale = 10.0 ** (0.5 * jax.random.uniform(key_cols, (GROUPS, SLOTS, 1, BS), jnp.float32))
    return (base * row_scale * col_scale).astype(jnp.bfloat16)


def draw_left_root(key, part):
    key = jax.random.fold_in(key, 2)
    return make_root(key).astype(jnp.bfloat16)


def draw_right_root(key, part):
    key = jax.random.fold_in(key, 3)
    return make_root(key).astype(jnp.bfloat16)


def plant(values, stream_key, smallest, largest):
    extent = values.shape
    spot = [jax.random.randint(jax.random.fold_in(stream_key, axis), (), 0, extent[axis]) for axis in range(len(extent))]
    values = values.at[tuple(spot)].set(smallest)
    longest = extent.index(max(extent))
    spot[longest] = (spot[longest] + 1) % extent[longest]
    return values.at[tuple(spot)].set(largest)


def setup_inputs(seed: int = 0) -> dict:
    key_list = jax.random.split(jax.random.key(seed), 6)
    gradient = draw_gradient(jax.random.fold_in(key_list[5], 71), 0)
    left_root = draw_left_root(jax.random.fold_in(key_list[5], 71), 0)
    right_root = draw_right_root(jax.random.fold_in(key_list[5], 71), 0)
    slot_table = jax.vmap(lambda own: jax.random.permutation(own, SLOTS))(jax.random.split(key_list[3], GROUPS)).reshape((GROUPS, SLOTS)).astype(jnp.int32)
    overflow = plant((jax.random.randint(key_list[4], (GROUPS, SLOTS, N_DP), 0, 128) < 1).astype(jnp.int32), jax.random.fold_in(key_list[4], 1), 0, 1)
    return {"gradient": gradient, "left_root": left_root, "right_root": right_root, "slot_table": slot_table, "overflow": overflow}


def reference(gradient, left_root, right_root, slot_table, overflow):
    keep_mask = (lax.optimization_barrier(jnp.max(overflow, axis=2)) == 0).astype(jnp.float32)

    def group_squares(grad_rows):
        return lax.optimization_barrier(jnp.sum(jnp.square(grad_rows.astype(jnp.float32)), axis=(1, 2)))
    squares = lax.map(group_squares, gradient)
    grand_total = jnp.sum(squares * keep_mask)
    clip_factor = jnp.minimum(jnp.float32(1.0), BS * math.sqrt(BLOCKS) / jnp.sqrt(grand_total + 1e-06))

    def one_group(group_args):
        grad_rows, lefts, rights, slot_of, keeps = group_args

        def one_block(block_args):
            block, slot, keep_one = block_args
            left_product = jnp.dot(lefts[slot], block, preferred_element_type=jnp.float32).astype(jnp.bfloat16)
            preconditioned = jnp.dot(left_product, rights[slot], preferred_element_type=jnp.float32)
            block_sq = jnp.sum(jnp.square(block.astype(jnp.float32)))
            pre_sq = jnp.sum(preconditioned * preconditioned)
            scaled = preconditioned * (jnp.sqrt(block_sq) / jnp.sqrt(pre_sq + 1e-06)) * keep_one * clip_factor
            return scaled.astype(jnp.bfloat16)
        return lax.map(one_block, (grad_rows, slot_of, keeps))
    return lax.map(one_group, (gradient, left_root, right_root, slot_table, keep_mask))
```

```python
import functools
import math

import jax
import jax.numpy as jnp
from jax import lax
from jax.experimental import pallas as pl
from jax.experimental.pallas import tpu as pltpu
from jax.sharding import PartitionSpec as P

MARK = 1e30
LIMIT = 1e29

LANES = 128
PART = 4
PIECES = 4

SMEM = pl.BlockSpec(memory_space=pltpu.SMEM)
VMEM = pl.BlockSpec(memory_space=pltpu.VMEM)
HBM = pl.BlockSpec(memory_space=pltpu.HBM)
AFTER_PARAMS = pltpu.CompilerParams(vmem_limit_bytes=63_200_000)
PARAMS = pltpu.CompilerParams(vmem_limit_bytes=32 * 1024 * 1024)


def sum_squares(flag_ref, grad_ref, partial_ref, lanes_ref):
    cols = grad_ref.shape[2]
    for b in range(lanes_ref.shape[0]):
        wide = grad_ref[b].astype(jnp.float32)
        square = wide * wide
        lane = square[:, 0:LANES]
        for c in range(LANES, cols, LANES):
            lane = lane + square[:, c : c + LANES]
        lane = jnp.sum(lane, axis=0, keepdims=True)
        flagged = flag_ref[0, b] != 0
        lanes_ref[b : b + 1, :] = jnp.where(flagged, jnp.full_like(lane, MARK), lane)
    partial_ref[...] = jnp.sum(lanes_ref[...].T, axis=0, keepdims=True)


def send_kernel(
    slot_hbm,
    flag_hbm,
    grad_hbm,
    rows_hbm,
    partial_hbm,
    slot_ref,
    flag_ref,
    tiles_ref,
    part_ref,
    lanes_ref,
    loads,
    sem,
):
    slots = rows_hbm.shape[0]
    tables = [
        pltpu.make_async_copy(slot_hbm, slot_ref, loads.at[PIECES]),
        pltpu.make_async_copy(flag_hbm, flag_ref, loads.at[PIECES + 1]),
    ]
    for copy in tables:
        copy.start()
    pieces = []
    for piece in range(PIECES):
        span = pl.ds(piece * slots // PIECES, slots // PIECES)
        pieces.append(
            pltpu.make_async_copy(grad_hbm.at[span], tiles_ref.at[span], loads.at[piece])
        )
        pieces[-1].start()
    tiles_ref[slots] = jnp.full(tiles_ref.shape[1:], jnp.inf, tiles_ref.dtype)
    for copy in tables:
        copy.wait()
    for piece in range(PIECES):
        pieces[piece].wait()
        for b in range(piece * slots // PIECES, (piece + 1) * slots // PIECES):
            flagged = flag_ref[0, b] != 0
            source = jnp.where(flagged, slots, b)
            pltpu.make_async_copy(
                tiles_ref.at[source], rows_hbm.at[slot_ref[0, b]], sem
            ).start()

    sum_squares(flag_ref, tiles_ref, part_ref, lanes_ref)
    part_copy = pltpu.make_async_copy(part_ref, partial_hbm, loads.at[PIECES])
    part_copy.start()
    pltpu.make_async_copy(tiles_ref.at[pl.ds(0, slots)], rows_hbm, sem).wait()
    part_copy.wait()


def after_kernel(rows_ref, swapped_ref, out_ref):
    del rows_ref, swapped_ref, out_ref


def block_kernel(block_ref, left_ref, right_ref, sums_ref, out_ref):
    slots, places = out_ref.shape[0:2]
    order, cols = block_ref.shape
    parts = order // (slots * PART)
    block = block_ref[...]
    wide = block.astype(jnp.float32)
    block_sq = jnp.sum(wide * wide, keepdims=True)
    keep = block_sq < LIMIT
    left_product = jnp.dot(left_ref[...], block, preferred_element_type=jnp.float32).astype(
        jnp.bfloat16
    )
    preconditioned = jnp.dot(left_product, right_ref[...], preferred_element_type=jnp.float32)
    pre_sq = jnp.sum(preconditioned * preconditioned, keepdims=True)
    ratio = jnp.sqrt(block_sq) / jnp.sqrt(pre_sq + 1e-06)
    scaled = jnp.where(keep, preconditioned * ratio, 0.0)
    for c in range(0, cols, LANES):
        tiles = scaled[:, c : c + LANES].reshape(slots, parts, PART, LANES).astype(jnp.bfloat16)
        place = c // LANES * parts
        out_ref[:, place : place + parts] = tiles
    sums = sums_ref[...].astype(jnp.bfloat16)
    both = jnp.concatenate([sums[0:PART], sums[PART : 2 * PART]], axis=1)
    for s in range(slots):
        out_ref[s, places - 1] = both


def finish_kernel(bound, slot_table_ref, rows_ref, out_hbm, slot_ref, out_ref, sems):
    slots, rows, cols = out_ref.shape
    table = pltpu.make_async_copy(slot_table_ref, slot_ref, sems.at[PIECES])
    table.start()
    parts = rows // PART
    owed = rows_ref[:, rows_ref.shape[1] - 1].astype(jnp.float32)
    squares = jnp.sum(owed, axis=0)
    grand_total = jnp.sum(jnp.where(squares < LIMIT, squares, 0.0), keepdims=True)
    clip = jnp.minimum(1.0, bound / jnp.sqrt(grand_total + 1e-06))
    table.wait()
    copies = []
    for piece in range(PIECES):
        first, last = piece * slots // PIECES, (piece + 1) * slots // PIECES
        for b in range(first, last):
            slot = slot_ref[0, b]
            for c in range(0, cols, LANES):
                place = c // LANES * parts
                tile = rows_ref[slot, place : place + parts].astype(jnp.float32)
                out_ref[b, :, c : c + LANES] = (tile.reshape(rows, LANES) * clip).astype(
                    jnp.bfloat16
                )
        span = pl.ds(first, last - first)
        copy = pltpu.make_async_copy(out_ref.at[span], out_hbm.at[span], sems.at[piece])
        copy.start()
        copies.append(copy)
    for copy in copies:
        copy.wait()


def swapped(value, size, core, step):
    return lax.ppermute(value, "mp", [(i, i ^ step) for i in range(core, size, 2)])


def on_device(n_mp, gradient, left_root, right_root, slot_table, overflow):
    slots, rows, cols = gradient.shape[1:]
    order = left_root.shape[-1]
    flags = overflow.reshape(1, slots)
    row_tiles, partial = pl.pallas_call(
        send_kernel,
        out_shape=(
            jax.ShapeDtypeStruct((slots, rows, cols), jnp.bfloat16),
            jax.ShapeDtypeStruct((1, slots), jnp.float32),
        ),
        in_specs=[HBM] * 3,
        out_specs=(HBM, HBM),
        scratch_shapes=[
            pltpu.SMEM((1, slots), jnp.int32),
            pltpu.SMEM((1, slots), jnp.int32),
            pltpu.VMEM((slots + 1, rows, cols), jnp.bfloat16),
            pltpu.VMEM((1, slots), jnp.float32),
            pltpu.VMEM((slots, LANES), jnp.float32),
            pltpu.SemaphoreType.DMA((PIECES + 2,)),
            pltpu.SemaphoreType.DMA,
        ],
        name="send",
    )(slot_table, flags, gradient[0])

    first = swapped(partial, n_mp, 0, 2)
    second = swapped(jnp.concatenate([partial, first], axis=0), n_mp, 0, 4)
    row_tiles = pl.pallas_call(
        after_kernel,
        out_shape=jax.ShapeDtypeStruct(row_tiles.shape, row_tiles.dtype),
        in_specs=[HBM, pl.BlockSpec(memory_space=pl.ANY)],
        out_specs=HBM,
        input_output_aliases={0: 0},
        compiler_params=AFTER_PARAMS,
        name="after",
    )(row_tiles, second)
    blocks = lax.all_to_all(row_tiles, "dp", split_axis=0, concat_axis=0, tiled=True)
    again = partial + second[0:1]
    first_1 = swapped(again, n_mp, 1, 2)
    second_1 = swapped(jnp.concatenate([again, first_1], axis=0), n_mp, 1, 4)
    own = jnp.concatenate([partial, first + first_1, second + second_1], axis=0)
    other = lax.ppermute(own, "mp", [(i, i ^ 1) for i in range(n_mp)])
    sums = jnp.concatenate([own, other], axis=0)

    places = order * cols // (slots * PART * LANES) + 1
    scaled = pl.pallas_call(
        block_kernel,
        out_shape=jax.ShapeDtypeStruct((slots, places, PART, LANES), jnp.bfloat16),
        in_specs=[VMEM] * 4,
        out_specs=VMEM,
        compiler_params=PARAMS,
        name="block",
    )(blocks.reshape(order, cols), left_root[0, 0], right_root[0, 0], sums)

    returned = lax.all_to_all(scaled, "dp", split_axis=0, concat_axis=0, tiled=True)
    result = pl.pallas_call(
        functools.partial(finish_kernel, order * math.sqrt(slots * n_mp)),
        out_shape=jax.ShapeDtypeStruct((slots, rows, cols), jnp.bfloat16),
        in_specs=[VMEM, VMEM],
        out_specs=HBM,
        scratch_shapes=[
            pltpu.SMEM((1, slots), jnp.int32),
            pltpu.VMEM((slots, rows, cols), jnp.bfloat16),
            pltpu.SemaphoreType.DMA((PIECES + 1,)),
        ],
        compiler_params=PARAMS,
        name="finish",
    )(slot_table, returned)
    return result[None]


def solution(mesh):
    return jax.shard_map(
        functools.partial(on_device, mesh.shape["mp"]),
        mesh=mesh,
        in_specs=(
            P("mp", None, "dp", None),
            P("mp", "dp", None, None),
            P("mp", "dp", None, None),
            P("mp", None),
            P("mp", None, "dp"),
        ),
        out_specs=P("mp", None, "dp", None),
        check_vma=False,
    )
```

```python
import functools
import math

import jax
import jax.numpy as jnp
from jax import lax
from jax.experimental import pallas as pl
from jax.experimental.pallas import tpu as pltpu
from jax.sharding import PartitionSpec as P

MARK = 1e30
LIMIT = 1e29

LANES = 128
PART = 4
PIECES = 4

SMEM = pl.BlockSpec(memory_space=pltpu.SMEM)
VMEM = pl.BlockSpec(memory_space=pltpu.VMEM)
HBM = pl.BlockSpec(memory_space=pltpu.HBM)
AFTER_PARAMS = pltpu.CompilerParams(vmem_limit_bytes=63_200_000)
PARAMS = pltpu.CompilerParams(vmem_limit_bytes=32 * 1024 * 1024)


def sum_squares(flag_ref, grad_ref, partial_ref, lanes_ref):
    cols = grad_ref.shape[2]
    for b in range(lanes_ref.shape[0]):
        wide = grad_ref[b].astype(jnp.float32)
        square = wide * wide
        lane = square[:, 0:LANES]
        for c in range(LANES, cols, LANES):
            lane = lane + square[:, c : c + LANES]
        lane = jnp.sum(lane, axis=0, keepdims=True)
        flagged = flag_ref[0, b] != 0
        lanes_ref[b : b + 1, :] = jnp.where(flagged, jnp.full_like(lane, MARK), lane)
    partial_ref[...] = jnp.sum(lanes_ref[...].T, axis=0, keepdims=True)


def send_kernel(
    slot_hbm,
    flag_hbm,
    grad_hbm,
    rows_hbm,
    partial_hbm,
    slot_ref,
    flag_ref,
    tiles_ref,
    part_ref,
    lanes_ref,
    loads,
    sem,
):
    slots = rows_hbm.shape[0]
    tables = [
        pltpu.make_async_copy(slot_hbm, slot_ref, loads.at[PIECES]),
        pltpu.make_async_copy(flag_hbm, flag_ref, loads.at[PIECES + 1]),
    ]
    for copy in tables:
        copy.start()
    pieces = []
    for piece in range(PIECES):
        span = pl.ds(piece * slots // PIECES, slots // PIECES)
        pieces.append(
            pltpu.make_async_copy(grad_hbm.at[span], tiles_ref.at[span], loads.at[piece])
        )
        pieces[-1].start()
    tiles_ref[slots] = jnp.full(tiles_ref.shape[1:], jnp.inf, tiles_ref.dtype)
    for copy in tables:
        copy.wait()
    for piece in range(PIECES):
        pieces[piece].wait()
        for b in range(piece * slots // PIECES, (piece + 1) * slots // PIECES):
            flagged = flag_ref[0, b] != 0
            source = jnp.where(flagged, slots, b)
            pltpu.make_async_copy(
                tiles_ref.at[source], rows_hbm.at[slot_ref[0, b]], sem
            ).start()

    sum_squares(flag_ref, tiles_ref, part_ref, lanes_ref)
    part_copy = pltpu.make_async_copy(part_ref, partial_hbm, loads.at[PIECES])
    part_copy.start()
    pltpu.make_async_copy(tiles_ref.at[pl.ds(0, slots)], rows_hbm, sem).wait()
    part_copy.wait()


def after_kernel(rows_ref, swapped_ref, out_ref):
    del rows_ref, swapped_ref, out_ref


def again_kernel(partial_ref, rows_ref, out_ref):
    del rows_ref
    out_ref[...] = partial_ref[...]


def block_kernel(block_ref, left_ref, right_ref, sums_ref, out_ref):
    slots, places = out_ref.shape[0:2]
    order, cols = block_ref.shape
    parts = order // (slots * PART)
    block = block_ref[...]
    wide = block.astype(jnp.float32)
    block_sq = jnp.sum(wide * wide, keepdims=True)
    keep = block_sq < LIMIT
    left_product = jnp.dot(left_ref[...], block, preferred_element_type=jnp.float32).astype(
        jnp.bfloat16
    )
    preconditioned = jnp.dot(left_product, right_ref[...], preferred_element_type=jnp.float32)
    pre_sq = jnp.sum(preconditioned * preconditioned, keepdims=True)
    ratio = jnp.sqrt(block_sq) / jnp.sqrt(pre_sq + 1e-06)
    scaled = jnp.where(keep, preconditioned * ratio, 0.0)
    for c in range(0, cols, LANES):
        tiles = scaled[:, c : c + LANES].reshape(slots, parts, PART, LANES).astype(jnp.bfloat16)
        place = c // LANES * parts
        out_ref[:, place : place + parts] = tiles
    sums = sums_ref[...].astype(jnp.bfloat16)
    both = jnp.concatenate([sums[0:PART], sums[PART : 2 * PART]], axis=1)
    for s in range(slots):
        out_ref[s, places - 1] = both


def finish_kernel(bound, slot_table_ref, rows_ref, out_hbm, slot_ref, out_ref, sems):
    slots, rows, cols = out_ref.shape
    table = pltpu.make_async_copy(slot_table_ref, slot_ref, sems.at[PIECES])
    table.start()
    parts = rows // PART
    owed = rows_ref[:, rows_ref.shape[1] - 1].astype(jnp.float32)
    squares = jnp.sum(owed, axis=0)
    grand_total = jnp.sum(jnp.where(squares < LIMIT, squares, 0.0), keepdims=True)
    clip = jnp.minimum(1.0, bound / jnp.sqrt(grand_total + 1e-06))
    table.wait()
    copies = []
    for piece in range(PIECES):
        first, last = piece * slots // PIECES, (piece + 1) * slots // PIECES
        for b in range(first, last):
            slot = slot_ref[0, b]
            for c in range(0, cols, LANES):
                place = c // LANES * parts
                tile = rows_ref[slot, place : place + parts].astype(jnp.float32)
                out_ref[b, :, c : c + LANES] = (tile.reshape(rows, LANES) * clip).astype(
                    jnp.bfloat16
                )
        span = pl.ds(first, last - first)
        copy = pltpu.make_async_copy(out_ref.at[span], out_hbm.at[span], sems.at[piece])
        copy.start()
        copies.append(copy)
    for copy in copies:
        copy.wait()


def swapped(value, size, core, step):
    return lax.ppermute(value, "mp", [(i, i ^ step) for i in range(core, size, 2)])


def on_device(n_mp, gradient, left_root, right_root, slot_table, overflow):
    slots, rows, cols = gradient.shape[1:]
    order = left_root.shape[-1]
    flags = overflow.reshape(1, slots)
    row_tiles, partial = pl.pallas_call(
        send_kernel,
        out_shape=(
            jax.ShapeDtypeStruct((slots, rows, cols), jnp.bfloat16),
            jax.ShapeDtypeStruct((1, slots), jnp.float32),
        ),
        in_specs=[HBM] * 3,
        out_specs=(HBM, HBM),
        scratch_shapes=[
            pltpu.SMEM((1, slots), jnp.int32),
            pltpu.SMEM((1, slots), jnp.int32),
            pltpu.VMEM((slots + 1, rows, cols), jnp.bfloat16),
            pltpu.VMEM((1, slots), jnp.float32),
            pltpu.VMEM((slots, LANES), jnp.float32),
            pltpu.SemaphoreType.DMA((PIECES + 2,)),
            pltpu.SemaphoreType.DMA,
        ],
        name="send",
    )(slot_table, flags, gradient[0])

    first = swapped(partial, n_mp, 0, 2)
    second = swapped(jnp.concatenate([partial, first], axis=0), n_mp, 0, 4)
    row_tiles = pl.pallas_call(
        after_kernel,
        out_shape=jax.ShapeDtypeStruct(row_tiles.shape, row_tiles.dtype),
        in_specs=[HBM, pl.BlockSpec(memory_space=pl.ANY)],
        out_specs=HBM,
        input_output_aliases={0: 0},
        compiler_params=AFTER_PARAMS,
        name="after",
    )(row_tiles, second)
    blocks = lax.all_to_all(row_tiles, "dp", split_axis=0, concat_axis=0, tiled=True)
    again = pl.pallas_call(
        again_kernel,
        out_shape=jax.ShapeDtypeStruct((1, slots), jnp.float32),
        in_specs=[VMEM, pl.BlockSpec(memory_space=pl.ANY)],
        out_specs=VMEM,
        compiler_params=PARAMS,
        name="again",
    )(partial, row_tiles)
    first_1 = swapped(again, n_mp, 1, 2)
    second_1 = swapped(jnp.concatenate([again, first_1], axis=0), n_mp, 1, 4)
    own = jnp.concatenate([again, first + first_1, second + second_1], axis=0)
    other = lax.ppermute(own, "mp", [(i, i ^ 1) for i in range(n_mp)])
    sums = jnp.concatenate([own, other], axis=0)

    places = order * cols // (slots * PART * LANES) + 1
    scaled = pl.pallas_call(
        block_kernel,
        out_shape=jax.ShapeDtypeStruct((slots, places, PART, LANES), jnp.bfloat16),
        in_specs=[VMEM] * 4,
        out_specs=VMEM,
        compiler_params=PARAMS,
        name="block",
    )(blocks.reshape(order, cols), left_root[0, 0], right_root[0, 0], sums)

    returned = lax.all_to_all(scaled, "dp", split_axis=0, concat_axis=0, tiled=True)
    result = pl.pallas_call(
        functools.partial(finish_kernel, order * math.sqrt(slots * n_mp)),
        out_shape=jax.ShapeDtypeStruct((slots, rows, cols), jnp.bfloat16),
        in_specs=[VMEM, VMEM],
        out_specs=HBM,
        scratch_shapes=[
            pltpu.SMEM((1, slots), jnp.int32),
            pltpu.VMEM((slots, rows, cols), jnp.bfloat16),
            pltpu.SemaphoreType.DMA((PIECES + 1,)),
        ],
        compiler_params=PARAMS,
        name="finish",
    )(slot_table, returned)
    return result[None]


def solution(mesh):
    return jax.shard_map(
        functools.partial(on_device, mesh.shape["mp"]),
        mesh=mesh,
        in_specs=(
            P("mp", None, "dp", None),
            P("mp", "dp", None, None),
            P("mp", "dp", None, None),
            P("mp", None),
            P("mp", None, "dp"),
        ),
        out_specs=P("mp", None, "dp", None),
        check_vma=False,
    )
```
